256 devices in a mesh: depth: 8 (over z_hi, core), tile: 32 (over z_lo, y, x).
Axes of the slice: x: 4, y: 4, z: 8 (z_hi: 4, z_lo: 2; z = z_hi * 2 + z_lo), core: 2. Of those that a mesh axis runs over, the one named last changes fastest.
Arguments:
- first_factor_embedding: bfloat16 [1024, 64, 32], P('depth', 'tile'), may hold values from -6 to 6
- second_factor_embedding: bfloat16 [1024, 3072, 32], P('depth', 'tile'), may hold values from -6 to 6
- final_linear_matrix: bfloat16 [1024, 128], replicated, may hold values from -4.1875 to 4.1875
- output_bias: float32 [128], replicated, may hold values from -3 to 3
Outputs:
- pair_update: bfloat16 [64, 3072, 128], P('depth', 'tile')
The draws below stay inside these ranges and needn't reach their ends.
All inputs are finite; a program needn't handle non-finite values.
Results may differ from the reference program's by a relative error of at most 0.01.
Values may be sent and summed in bfloat16 or wider, within the bound.
No kernel may reach another device: no remote copies, remote signals or barrier semaphores. Data moves between devices by JAX's collectives and lax.ppermute only.
A program may use at most 192 MiB of HBM per device.

```python
import jax
import jax.numpy as jnp
from jax import lax

FEATURE_DEPTH = 32
COUPLING_FEATS = 128
STRIP_LINES = 64
HOMOLOG_TOTAL = 1024
AMINO_TOTAL = 3072


def block_levels(stream_key, dims, split, low, high):
    gain = 1.0
    for position, blocks in split:
        draws = jax.random.uniform(jax.random.fold_in(jax.random.fold_in(stream_key, 6), position), (blocks,), jnp.float32, low / len(split), high / len(split))
        gain = gain * jnp.repeat(jnp.exp(draws), dims[position] // blocks).reshape((-1,) + (1,) * (len(dims) - 1 - position))
    return gain


def noise(stream_key, extent, width, most, shards=(), dtype=jnp.bfloat16):
    level = block_levels(stream_key, extent, shards, -0.22, 0.18) if shards else 1.0
    result = jax.random.normal(stream_key, extent, jnp.float32) * width * level
    return jnp.minimum(jnp.maximum(result, -most), most).astype(dtype)


def setup_inputs(seed: int = 0) -> dict:
    key_list = jax.random.split(jax.random.key(seed), 5)
    first_factor_embedding = noise(key_list[0], (HOMOLOG_TOTAL, STRIP_LINES, FEATURE_DEPTH), 1.0, 6.0, ((0, 8), (1, 32)))
    second_factor_embedding = noise(key_list[1], (HOMOLOG_TOTAL, AMINO_TOTAL, FEATURE_DEPTH), 1.0, 6.0, ((0, 8), (1, 32)))
    final_linear_matrix = noise(key_list[2], (FEATURE_DEPTH * FEATURE_DEPTH, COUPLING_FEATS), 0.7, 4.1875)
    output_bias = noise(key_list[3], (COUPLING_FEATS,), 0.5, 3.0, (), jnp.float32)
    return dict(first_factor_embedding=first_factor_embedding, second_factor_embedding=second_factor_embedding, final_linear_matrix=final_linear_matrix, output_bias=output_bias)


def reference(first_factor_embedding, second_factor_embedding, final_linear_matrix, output_bias):
    weight = final_linear_matrix.astype(jnp.float32)
    right_flattened = second_factor_embedding.astype(jnp.float32)

    def single_row(column):
        averaged_tensor_coupling = jnp.einsum("sc,sje->jce", column.astype(jnp.float32), right_flattened, precision=lax.Precision.HIGHEST)
        averaged_tensor_coupling = averaged_tensor_coupling.reshape(AMINO_TOTAL, FEATURE_DEPTH * FEATURE_DEPTH) / HOMOLOG_TOTAL
        mixed = jnp.dot(averaged_tensor_coupling, weight, precision=lax.Precision.HIGHEST) + output_bias
        return mixed.astype(jnp.bfloat16)

    return lax.map(single_row, jnp.swapaxes(first_factor_embedding, 0, 1))
```

```python
import functools

import jax
import jax.numpy as jnp
from jax import lax
from jax.experimental import pallas as pl
from jax.experimental.pallas import tpu as pltpu
from jax.sharding import Mesh, PartitionSpec as P

FEATS = 32
ROWS = 8
LANES = 128
RING = 4
DEPTH_AXES = ("zh", "core")
TILE_AXES = ("zl", "y", "x")


def prep_kernel(own_ref, other_ref, out_ref, wide_ref):
    cols = own_ref.shape[0] // FEATS
    for half, ref in ((0, own_ref), (1, other_ref)):
        wide_ref[...] = ref[...].astype(jnp.float32)
        for f in range(FEATS):
            picked = wide_ref[pl.ds(f, cols, stride=FEATS), :]
            out_ref[f, 0:cols, half * LANES:(half + 1) * LANES] = picked.astype(jnp.bfloat16)
    out_ref[:, cols:, :] = jnp.zeros((FEATS, LANES - cols, 2 * LANES), jnp.bfloat16)


def prep(own, other):
    cols = own.shape[0]
    whole = pl.BlockSpec(memory_space=pltpu.VMEM)
    return pl.pallas_call(
        prep_kernel,
        out_shape=jax.ShapeDtypeStruct((FEATS, LANES, 2 * LANES), jnp.bfloat16),
        scratch_shapes=[pltpu.VMEM((cols * FEATS, LANES), jnp.float32)],
        in_specs=[whole, whole],
        out_specs=whole,
        compiler_params=pltpu.CompilerParams(vmem_limit_bytes=32 << 20),
        cost_estimate=pl.CostEstimate(flops=0, bytes_accessed=8 << 20, transcendentals=0),
        name="prep",
    )(own.reshape(cols * FEATS, LANES), other.reshape(cols * FEATS, LANES))


def pair_kernel(chunks, idx_ref, own_ref, other_ref, b_ref, w_ref, out_ref):
    width = ROWS * FEATS
    a = jnp.concatenate(
        [own_ref[...].reshape(width, LANES), other_ref[...].reshape(width, LANES)], axis=1
    )
    feats = FEATS // chunks
    total = None
    for c in range(chunks):
        b = b_ref[c * feats:(c + 1) * feats].reshape(feats * LANES, 2 * LANES)
        outer = lax.dot_general(
            a, b, (((1,), (1,)), ((), ())), preferred_element_type=jnp.float32
        ).astype(jnp.bfloat16)
        stacked = jnp.concatenate(
            [
                jnp.concatenate(
                    [
                        outer[r * FEATS:(r + 1) * FEATS, f * LANES:(f + 1) * LANES]
                        for r in range(ROWS)
                    ],
                    axis=1,
                )
                for f in range(feats)
            ],
            axis=0,
        )
        lanes = feats * FEATS
        part = jnp.dot(
            w_ref[:, c * lanes:(c + 1) * lanes], stacked, preferred_element_type=jnp.float32
        )
        total = part if total is None else total + part
    cols = out_ref.shape[1]
    for r in range(ROWS):
        out_ref[r] = total[:, r * LANES:(r + 1) * LANES].T[:cols].astype(jnp.bfloat16)


def pair_block(idx, own, other, b, wt, cols):
    rows = pl.BlockSpec(
        (None, None, ROWS, FEATS, LANES), lambda i, idx: (idx[0], idx[1], 0, 0, 0)
    )
    return pl.pallas_call(
        functools.partial(pair_kernel, 4),
        grid_spec=pltpu.PrefetchScalarGridSpec(
            num_scalar_prefetch=1,
            grid=(1,),
            in_specs=[
                rows,
                rows,
                pl.BlockSpec(b.shape, lambda i, idx: (0, 0, 0)),
                pl.BlockSpec(wt.shape, lambda i, idx: (0, 0)),
            ],
            out_specs=pl.BlockSpec((ROWS, cols, LANES), lambda i, idx: (0, 0, 0)),
        ),
        out_shape=jax.ShapeDtypeStruct((ROWS, cols, LANES), jnp.bfloat16),
        compiler_params=pltpu.CompilerParams(vmem_limit_bytes=40 << 20),
        cost_estimate=pl.CostEstimate(flops=3 << 30, bytes_accessed=4 << 20, transcendentals=0),
        name="pair_block",
    )(idx, own, other, b, wt)


def local(first, second, matrix, bias):
    tiles = 32
    sequences = 1024
    swap = [(0, 1), (1, 0)]
    zh = lax.axis_index("zh")
    core = lax.axis_index("core")
    at = jnp.transpose(first, (1, 2, 0))
    bt = jnp.transpose(second, (1, 2, 0))
    cols = bt.shape[0]
    b_other = lax.ppermute(bt, "core", swap)
    spread = jnp.broadcast_to(at[None], (tiles,) + at.shape)
    a_own = lax.all_to_all(spread, TILE_AXES, split_axis=0, concat_axis=0, tiled=True)
    a_own = a_own.reshape(RING, 2, ROWS, FEATS, LANES)
    a_other = lax.ppermute(a_own, "core", swap)
    b = prep(bt, b_other)
    wt = matrix.reshape(FEATS, FEATS, LANES).transpose(2, 1, 0).reshape(LANES, FEATS * FEATS)

    def block(k):
        idx = jnp.stack([(zh + k) % RING, core]).astype(jnp.int32)
        return pair_block(idx, a_own, a_other, b, wt, cols)

    total = None
    received = []
    for k in (2, 1, 3):
        part = block(k)
        received.append(lax.ppermute(part, "zh", [(i, (i + k) % RING) for i in range(RING)]))
    total = block(0).astype(jnp.float32)
    for part in received:
        total = total + part.astype(jnp.float32)
    return (total * (1.0 / sequences) + bias).astype(jnp.bfloat16)


def solution(mesh):
    fine = Mesh(
        mesh.devices.reshape(RING, 2, 2, 4, 4), DEPTH_AXES + TILE_AXES
    )
    in_specs = (P(DEPTH_AXES, TILE_AXES, None), P(DEPTH_AXES, TILE_AXES, None), P(), P())
    out_specs = P(DEPTH_AXES, TILE_AXES, None)
    return jax.shard_map(local, mesh=fine, in_specs=in_specs, out_specs=out_specs, check_vma=False)
```

```python
import functools

import jax
import jax.numpy as jnp
from jax import lax
from jax.experimental import pallas as pl
from jax.experimental.pallas import tpu as pltpu
from jax.sharding import Mesh, PartitionSpec as P

FEATS = 32
ROWS = 8
LANES = 128
RING = 4
TILES = 32
DEPTH_AXES = ("zh", "core")
TILE_AXES = ("zl", "y", "x")
SWAP = [(0, 1), (1, 0)]
WHOLE = pl.BlockSpec(memory_space=pltpu.VMEM)
ANY = pl.BlockSpec(memory_space=pltpu.HBM)


def limit(mib):
    return pltpu.CompilerParams(vmem_limit_bytes=mib << 20)


def cost(nbytes, flops=0):
    return pl.CostEstimate(flops=flops, bytes_accessed=nbytes, transcendentals=0)


def spread_kernel(in_ref, out_ref, held_ref, filled_ref, in_sem, out_sem):
    fetch = pltpu.make_async_copy(in_ref, held_ref, in_sem)
    fetch.start()
    fetch.wait()
    own = held_ref[...]
    for t in range(TILES):
        filled_ref[t] = own
    store = pltpu.make_async_copy(filled_ref, out_ref, out_sem)
    store.start()
    store.wait()


def spread(own):
    return pl.pallas_call(
        spread_kernel,
        out_shape=jax.ShapeDtypeStruct((TILES,) + own.shape, jnp.bfloat16),
        in_specs=[ANY],
        out_specs=ANY,
        scratch_shapes=[
            pltpu.VMEM(own.shape, jnp.bfloat16),
            pltpu.VMEM((TILES,) + own.shape, jnp.bfloat16),
            pltpu.SemaphoreType.DMA,
            pltpu.SemaphoreType.DMA,
        ],
        compiler_params=limit(60),
        cost_estimate=cost(1 << 20),
        name="spread",
    )(own)


def turn(ref, wide_ref, out_ref):
    cols = ref.shape[0] // FEATS
    pad = jnp.zeros((LANES - cols, LANES), jnp.float32)
    wide_ref[...] = ref[...].astype(jnp.float32)
    for f in range(FEATS):
        picked = jnp.concatenate([wide_ref[pl.ds(f, cols, stride=FEATS), :], pad], axis=0)
        out_ref[0:LANES, f * LANES:(f + 1) * LANES] = picked.T.astype(jnp.bfloat16)


def own_kernel(b_ref, matrix_ref, out_ref, wide_ref, matrix_wide_ref, matrix_held_ref, sem):
    fetch = pltpu.make_async_copy(matrix_ref, matrix_held_ref, sem)
    fetch.start()
    turn(b_ref, wide_ref, out_ref)
    fetch.wait()
    matrix_wide_ref[...] = matrix_held_ref[...].astype(jnp.float32)
    group = LANES // FEATS
    for g in range(FEATS // group):
        rows = [
            matrix_wide_ref[pl.ds(g * group + i, FEATS, stride=FEATS), :] for i in range(group)
        ]
        out_ref[LANES:, g * LANES:(g + 1) * LANES] = jnp.concatenate(rows, axis=0).T.astype(
            jnp.bfloat16
        )


def turn_own(b, matrix):
    wide = (b.shape[0] * FEATS, LANES)
    return pl.pallas_call(
        own_kernel,
        out_shape=jax.ShapeDtypeStruct((2 * LANES, FEATS * LANES), jnp.bfloat16),
        scratch_shapes=[
            pltpu.VMEM(wide, jnp.float32),
            pltpu.VMEM(matrix.shape, jnp.float32),
            pltpu.VMEM(matrix.shape, jnp.bfloat16),
            pltpu.SemaphoreType.DMA,
        ],
        in_specs=[WHOLE, ANY],
        out_specs=WHOLE,
        compiler_params=limit(8),
        cost_estimate=cost(4 << 20),
        name="turn_own",
    )(b.reshape(wide), matrix)


def other_kernel(b_ref, out_ref, wide_ref):
    turn(b_ref, wide_ref, out_ref)


def turn_other(b):
    wide = (b.shape[0] * FEATS, LANES)
    return pl.pallas_call(
        other_kernel,
        out_shape=jax.ShapeDtypeStruct((LANES, FEATS * LANES), jnp.bfloat16),
        scratch_shapes=[pltpu.VMEM(wide, jnp.float32)],
        in_specs=[WHOLE],
        out_specs=WHOLE,
        compiler_params=limit(8),
        cost_estimate=cost(4 << 20),
        name="turn_other",
    )(b.reshape(wide))


def pair_kernel(hops, groups, own_ref, other_ref, b_own_ref, b_other_ref, out_ref, stack_ref):
    zh = lax.axis_index("zh")
    core = lax.axis_index("core")
    block = (zh + jnp.where(core == 0, hops[0], hops[1])) & (RING - 1)
    width = ROWS * FEATS
    parts = []
    for g in range(groups):
        half = core if g == 0 else 1 - core
        parts.append(
            jnp.concatenate(
                [
                    own_ref[block, half].reshape(width, LANES),
                    other_ref[block, half].reshape(width, LANES),
                ],
                axis=1,
            )
        )
    a = parts[0] if groups == 1 else jnp.concatenate(parts, axis=0)
    rows = ROWS * groups
    feats = 4
    for c in range(FEATS // feats):
        lanes = slice(c * feats * LANES, (c + 1) * feats * LANES)
        b = jnp.concatenate([b_own_ref[0:LANES, lanes], b_other_ref[:, lanes]], axis=0)
        outer = jnp.dot(a, b, preferred_element_type=jnp.float32).astype(jnp.bfloat16)
        for f in range(feats):
            k = (c * feats + f) * FEATS
            for r in range(rows):
                stack_ref[k:k + FEATS, r * LANES:(r + 1) * LANES] = outer[
                    r * FEATS:(r + 1) * FEATS, f * LANES:(f + 1) * LANES
                ]
    cols = out_ref.shape[1]
    w = b_own_ref[LANES:, 0:FEATS * FEATS]
    for r in range(0, rows, 2):
        mixed = jnp.dot(
            w, stack_ref[:, r * LANES:(r + 2) * LANES], preferred_element_type=jnp.float32
        )
        out_ref[r] = mixed[:, :LANES].T[:cols].astype(jnp.bfloat16)
        out_ref[r + 1] = mixed[:, LANES:].T[:cols].astype(jnp.bfloat16)


def pair_block(hops, groups, own, other, b_own, b_other, cols, flops=3 << 30):
    rows = ROWS * groups
    return pl.pallas_call(
        functools.partial(pair_kernel, hops, groups),
        out_shape=jax.ShapeDtypeStruct((rows, cols, LANES), jnp.bfloat16),
        in_specs=[WHOLE] * 4,
        out_specs=WHOLE,
        scratch_shapes=[pltpu.VMEM((FEATS * FEATS, rows * LANES), jnp.bfloat16)],
        compiler_params=limit(16),
        cost_estimate=cost(4 << 20, flops),
        name="pair_block",
    )(own, other, b_own, b_other)


def send(part, hops):
    pairs = []
    for z in range(RING):
        for c in range(2):
            pairs.append((z * 2 + c, (z + hops[c]) % RING * 2 + c))
    return lax.ppermute(part, DEPTH_AXES, pairs)


def local(first, second, matrix, bias):
    sequences = first.shape[0] * 2 * RING
    at = jnp.transpose(first, (1, 2, 0))
    bt = jnp.transpose(second, (1, 2, 0))
    cols = bt.shape[0]
    copies = spread(at)
    b_swapped = lax.ppermute(bt, "core", SWAP)
    a_own = lax.all_to_all(copies, TILE_AXES, split_axis=0, concat_axis=0, tiled=True)
    a_own = a_own.reshape(RING, 2, ROWS, FEATS, LANES)
    b_own = turn_own(bt, matrix)
    b_other = turn_other(b_swapped)
    a_swap, _ = lax.optimization_barrier((a_own, b_other))
    a_other = lax.ppermute(a_swap, "core", SWAP)
    block = functools.partial(
        pair_block, own=a_own, other=a_other, b_own=b_own, b_other=b_other, cols=cols
    )
    received = [send(block(hops, 1), hops) for hops in ((1, 3), (2, 2), (3, 1))]
    kept = block((0, 0), 1)
    parts = [kept] + received
    total = sum(part.astype(jnp.float32) for part in parts)
    return (total * (1.0 / sequences) + bias).astype(jnp.bfloat16)


def solution(mesh):
    fine = Mesh(mesh.devices.reshape(RING, 2, 2, 4, 4), DEPTH_AXES + TILE_AXES)
    in_specs = (P(DEPTH_AXES, TILE_AXES, None), P(DEPTH_AXES, TILE_AXES, None), P(), P())
    out_specs = P(DEPTH_AXES, TILE_AXES, None)
    return jax.shard_map(local, mesh=fine, in_specs=in_specs, out_specs=out_specs, check_vma=False)
```

```python
import functools

import jax
import jax.numpy as jnp
from jax import lax
from jax.experimental import pallas as pl
from jax.experimental.pallas import tpu as pltpu
from jax.sharding import Mesh, PartitionSpec as P

FEATS = 32
ROWS = 8
LANES = 128
RING = 4
TILES = 32
DEPTH_AXES = ("zh", "core")
TILE_AXES = ("zl", "y", "x")
SWAP = [(0, 1), (1, 0)]
WHOLE = pl.BlockSpec(memory_space=pltpu.VMEM)
ANY = pl.BlockSpec(memory_space=pltpu.HBM)


def limit(mib):
    return pltpu.CompilerParams(vmem_limit_bytes=mib << 20)


def cost(nbytes, flops=0):
    return pl.CostEstimate(flops=flops, bytes_accessed=nbytes, transcendentals=0)


def spread_kernel(in_ref, out_ref, held_ref, filled_ref, in_sem, out_sem):
    fetch = pltpu.make_async_copy(in_ref, held_ref, in_sem)
    fetch.start()
    fetch.wait()
    own = held_ref[...]
    for t in range(TILES):
        filled_ref[t] = own
    store = pltpu.make_async_copy(filled_ref, out_ref, out_sem)
    store.start()
    store.wait()


def spread(own):
    return pl.pallas_call(
        spread_kernel,
        out_shape=jax.ShapeDtypeStruct((TILES,) + own.shape, jnp.bfloat16),
        in_specs=[ANY],
        out_specs=ANY,
        scratch_shapes=[
            pltpu.VMEM(own.shape, jnp.bfloat16),
            pltpu.VMEM((TILES,) + own.shape, jnp.bfloat16),
            pltpu.SemaphoreType.DMA,
            pltpu.SemaphoreType.DMA,
        ],
        compiler_params=limit(60),
        cost_estimate=cost(1 << 20),
        name="spread",
    )(own)


def turn(ref, wide_ref, out_ref):
    cols = ref.shape[0] // FEATS
    pad = jnp.zeros((LANES - cols, LANES), jnp.float32)
    wide_ref[...] = ref[...].astype(jnp.float32)
    for f in range(FEATS):
        picked = jnp.concatenate([wide_ref[pl.ds(f, cols, stride=FEATS), :], pad], axis=0)
        out_ref[0:LANES, f * LANES:(f + 1) * LANES] = picked.T.astype(jnp.bfloat16)


def own_kernel(b_ref, matrix_ref, out_ref, wide_ref, matrix_wide_ref, matrix_held_ref, sem):
    fetch = pltpu.make_async_copy(matrix_ref, matrix_held_ref, sem)
    fetch.start()
    turn(b_ref, wide_ref, out_ref)
    fetch.wait()
    matrix_wide_ref[...] = matrix_held_ref[...].astype(jnp.float32)
    group = LANES // FEATS
    for g in range(FEATS // group):
        rows = [
            matrix_wide_ref[pl.ds(g * group + i, FEATS, stride=FEATS), :] for i in range(group)
        ]
        out_ref[LANES:, g * LANES:(g + 1) * LANES] = jnp.concatenate(rows, axis=0).T.astype(
            jnp.bfloat16
        )


def turn_own(b, matrix):
    wide = (b.shape[0] * FEATS, LANES)
    return pl.pallas_call(
        own_kernel,
        out_shape=jax.ShapeDtypeStruct((2 * LANES, FEATS * LANES), jnp.bfloat16),
        scratch_shapes=[
            pltpu.VMEM(wide, jnp.float32),
            pltpu.VMEM(matrix.shape, jnp.float32),
            pltpu.VMEM(matrix.shape, jnp.bfloat16),
            pltpu.SemaphoreType.DMA,
        ],
        in_specs=[WHOLE, ANY],
        out_specs=WHOLE,
        compiler_params=limit(8),
        cost_estimate=cost(4 << 20),
        name="turn_own",
    )(b.reshape(wide), matrix)


def other_kernel(b_ref, out_ref, wide_ref):
    turn(b_ref, wide_ref, out_ref)


def turn_other(b):
    wide = (b.shape[0] * FEATS, LANES)
    return pl.pallas_call(
        other_kernel,
        out_shape=jax.ShapeDtypeStruct((LANES, FEATS * LANES), jnp.bfloat16),
        scratch_shapes=[pltpu.VMEM(wide, jnp.float32)],
        in_specs=[WHOLE],
        out_specs=WHOLE,
        compiler_params=limit(8),
        cost_estimate=cost(4 << 20),
        name="turn_other",
    )(b.reshape(wide))


def pair_kernel(hops, groups, own_ref, other_ref, b_own_ref, b_other_ref, out_ref, stack_ref):
    zh = lax.axis_index("zh")
    core = lax.axis_index("core")
    block = (zh + jnp.where(core == 0, hops[0], hops[1])) & (RING - 1)
    width = ROWS * FEATS
    parts = []
    for g in range(groups):
        half = core if g == 0 else 1 - core
        parts.append(
            jnp.concatenate(
                [
                    own_ref[block, half].reshape(width, LANES),
                    other_ref[block, half].reshape(width, LANES),
                ],
                axis=1,
            )
        )
    a = parts[0] if groups == 1 else jnp.concatenate(parts, axis=0)
    rows = ROWS * groups
    feats = 4
    for c in range(FEATS // feats):
        lanes = slice(c * feats * LANES, (c + 1) * feats * LANES)
        b = jnp.concatenate([b_own_ref[0:LANES, lanes], b_other_ref[:, lanes]], axis=0)
        outer = jnp.dot(a, b, preferred_element_type=jnp.float32).astype(jnp.bfloat16)
        for f in range(feats):
            k = (c * feats + f) * FEATS
            for r in range(rows):
                stack_ref[k:k + FEATS, r * LANES:(r + 1) * LANES] = outer[
                    r * FEATS:(r + 1) * FEATS, f * LANES:(f + 1) * LANES
                ]
    cols = out_ref.shape[1]
    w = b_own_ref[LANES:, 0:FEATS * FEATS]
    for r in range(0, rows, 2):
        mixed = jnp.dot(
            w, stack_ref[:, r * LANES:(r + 2) * LANES], preferred_element_type=jnp.float32
        )
        out_ref[r] = mixed[:, :LANES].T[:cols].astype(out_ref.dtype)
        out_ref[r + 1] = mixed[:, LANES:].T[:cols].astype(out_ref.dtype)


def pair_block(hops, groups, own, other, b_own, b_other, cols, dtype=jnp.bfloat16):
    rows = ROWS * groups
    return pl.pallas_call(
        functools.partial(pair_kernel, hops, groups),
        out_shape=jax.ShapeDtypeStruct((rows, cols, LANES), dtype),
        in_specs=[WHOLE] * 4,
        out_specs=WHOLE,
        scratch_shapes=[pltpu.VMEM((FEATS * FEATS, rows * LANES), jnp.bfloat16)],
        compiler_params=limit(16),
        cost_estimate=cost(4 << 20, 3 << 30),
        name="pair_block",
    )(own, other, b_own, b_other)


def add_kernel(kept_ref, came_ref, out_ref):
    out_ref[...] = (kept_ref[...] + came_ref[...].astype(jnp.float32)).astype(out_ref.dtype)


def add_to(kept, came, dtype, name):
    return pl.pallas_call(
        add_kernel,
        out_shape=jax.ShapeDtypeStruct(kept.shape, dtype),
        in_specs=[WHOLE, WHOLE],
        out_specs=WHOLE,
        compiler_params=limit(8),
        cost_estimate=cost(200 << 20),
        name=name,
    )(kept, came)


def send(part, hops):
    pairs = []
    for z in range(RING):
        for c in range(2):
            pairs.append((z * 2 + c, (z + hops[c]) % RING * 2 + c))
    return lax.ppermute(part, DEPTH_AXES, pairs)


def local(first, second, matrix, bias):
    sequences = first.shape[0] * 2 * RING
    at = jnp.transpose(first, (1, 2, 0))
    bt = jnp.transpose(second, (1, 2, 0))
    cols = bt.shape[0]
    copies = spread(at)
    b_swapped = lax.ppermute(bt, "core", SWAP)
    a_own = lax.all_to_all(copies, TILE_AXES, split_axis=0, concat_axis=0, tiled=True)
    a_own = a_own.reshape(RING, 2, ROWS, FEATS, LANES)
    b_own = turn_own(bt, matrix)
    b_other = turn_other(b_swapped)
    a_swap, _ = lax.optimization_barrier((a_own, b_other))
    a_other = lax.ppermute(a_swap, "core", SWAP)
    block = functools.partial(
        pair_block, own=a_own, other=a_other, b_own=b_own, b_other=b_other, cols=cols
    )
    far = send(block((2, 2), 1), (1, 3))
    right = send(block((3, 1), 1), (3, 1))
    left_part = block((1, 3), 1, dtype=jnp.float32)
    kept = block((0, 0), 1, dtype=jnp.float32)
    far, kept, left_part = lax.optimization_barrier((far, kept, left_part))
    left = send(add_to(left_part, far, jnp.bfloat16, "merge"), (1, 3))
    total = add_to(kept, right, jnp.float32, "presum") + left.astype(jnp.float32)
    return (total * (1.0 / sequences) + bias).astype(jnp.bfloat16)


def solution(mesh):
    fine = Mesh(mesh.devices.reshape(RING, 2, 2, 4, 4), DEPTH_AXES + TILE_AXES)
    in_specs = (P(DEPTH_AXES, TILE_AXES, None), P(DEPTH_AXES, TILE_AXES, None), P(), P())
    out_specs = P(DEPTH_AXES, TILE_AXES, None)
    return jax.shard_map(local, mesh=fine, in_specs=in_specs, out_specs=out_specs, check_vma=False)
```

```python
import functools

import jax
import jax.numpy as jnp
from jax import lax
from jax.experimental import pallas as pl
from jax.experimental.pallas import tpu as pltpu
from jax.sharding import Mesh, PartitionSpec as P

FEATS = 32
ROWS = 8
LANES = 128
RING = 4
TILES = 32
DEPTH_AXES = ("zh", "core")
TILE_AXES = ("zl", "y", "x")
SWAP = [(0, 1), (1, 0)]
WHOLE = pl.BlockSpec(memory_space=pltpu.VMEM)
ANY = pl.BlockSpec(memory_space=pltpu.HBM)


def limit(mib):
    return pltpu.CompilerParams(vmem_limit_bytes=mib << 20)


def cost(nbytes, flops=0):
    return pl.CostEstimate(flops=flops, bytes_accessed=nbytes, transcendentals=0)


def spread_kernel(in_ref, out_ref, held_ref, filled_ref, in_sem, out_sem):
    fetch = pltpu.make_async_copy(in_ref, held_ref, in_sem)
    fetch.start()
    fetch.wait()
    own = held_ref[...]
    for t in range(TILES):
        filled_ref[t] = own
    store = pltpu.make_async_copy(filled_ref, out_ref, out_sem)
    store.start()
    store.wait()


def spread(own):
    return pl.pallas_call(
        spread_kernel,
        out_shape=jax.ShapeDtypeStruct((TILES,) + own.shape, jnp.bfloat16),
        in_specs=[ANY],
        out_specs=ANY,
        scratch_shapes=[
            pltpu.VMEM(own.shape, jnp.bfloat16),
            pltpu.VMEM((TILES,) + own.shape, jnp.bfloat16),
            pltpu.SemaphoreType.DMA,
            pltpu.SemaphoreType.DMA,
        ],
        compiler_params=limit(60),
        cost_estimate=cost(1 << 20),
        name="spread",
    )(own)


def turn(ref, wide_ref, out_ref):
    cols = ref.shape[0] // FEATS
    pad = jnp.zeros((LANES - cols, LANES), jnp.float32)
    wide_ref[...] = ref[...].astype(jnp.float32)
    for f in range(FEATS):
        picked = jnp.concatenate([wide_ref[pl.ds(f, cols, stride=FEATS), :], pad], axis=0)
        out_ref[0:LANES, f * LANES:(f + 1) * LANES] = picked.T.astype(jnp.bfloat16)


def own_kernel(b_ref, matrix_ref, out_ref, wide_ref, matrix_wide_ref, matrix_held_ref, sem):
    fetch = pltpu.make_async_copy(matrix_ref, matrix_held_ref, sem)
    fetch.start()
    turn(b_ref, wide_ref, out_ref)
    fetch.wait()
    matrix_wide_ref[...] = matrix_held_ref[...].astype(jnp.float32)
    group = LANES // FEATS
    for g in range(FEATS // group):
        rows = [
            matrix_wide_ref[pl.ds(g * group + i, FEATS, stride=FEATS), :] for i in range(group)
        ]
        out_ref[LANES:, g * LANES:(g + 1) * LANES] = jnp.concatenate(rows, axis=0).T.astype(
            jnp.bfloat16
        )


def turn_own(b, matrix):
    wide = (b.shape[0] * FEATS, LANES)
    return pl.pallas_call(
        own_kernel,
        out_shape=jax.ShapeDtypeStruct((2 * LANES, FEATS * LANES), jnp.bfloat16),
        scratch_shapes=[
            pltpu.VMEM(wide, jnp.float32),
            pltpu.VMEM(matrix.shape, jnp.float32),
            pltpu.VMEM(matrix.shape, jnp.bfloat16),
            pltpu.SemaphoreType.DMA,
        ],
        in_specs=[WHOLE, ANY],
        out_specs=WHOLE,
        compiler_params=limit(8),
        cost_estimate=cost(4 << 20),
        name="turn_own",
    )(b.reshape(wide), matrix)


def other_kernel(b_ref, out_ref, wide_ref):
    turn(b_ref, wide_ref, out_ref)


def turn_other(b):
    wide = (b.shape[0] * FEATS, LANES)
    return pl.pallas_call(
        other_kernel,
        out_shape=jax.ShapeDtypeStruct((LANES, FEATS * LANES), jnp.bfloat16),
        scratch_shapes=[pltpu.VMEM(wide, jnp.float32)],
        in_specs=[WHOLE],
        out_specs=WHOLE,
        compiler_params=limit(8),
        cost_estimate=cost(4 << 20),
        name="turn_other",
    )(b.reshape(wide))


def pair_kernel(hops, flip, own_ref, other_ref, b_own_ref, b_other_ref, out_ref, stack_ref):
    zh = lax.axis_index("zh")
    core = lax.axis_index("core")
    block = (zh + jnp.where(core == 0, hops[0], hops[1])) & (RING - 1)
    half = 1 - core if flip else core
    width = ROWS * FEATS
    a = jnp.concatenate(
        [
            own_ref[block, half].reshape(width, LANES),
            other_ref[block, half].reshape(width, LANES),
        ],
        axis=1,
    )
    feats = 4
    for c in range(FEATS // feats):
        lanes = slice(c * feats * LANES, (c + 1) * feats * LANES)
        b = jnp.concatenate([b_own_ref[0:LANES, lanes], b_other_ref[:, lanes]], axis=0)
        outer = jnp.dot(a, b, preferred_element_type=jnp.float32).astype(jnp.bfloat16)
        for f in range(feats):
            k = (c * feats + f) * FEATS
            for r in range(ROWS):
                stack_ref[k:k + FEATS, r * LANES:(r + 1) * LANES] = outer[
                    r * FEATS:(r + 1) * FEATS, f * LANES:(f + 1) * LANES
                ]
    cols = out_ref.shape[1]
    w = b_own_ref[LANES:, 0:FEATS * FEATS]
    for r in range(0, ROWS, 2):
        mixed = jnp.dot(
            w, stack_ref[:, r * LANES:(r + 2) * LANES], preferred_element_type=jnp.float32
        )
        out_ref[r] = mixed[:, :LANES].T[:cols].astype(out_ref.dtype)
        out_ref[r + 1] = mixed[:, LANES:].T[:cols].astype(out_ref.dtype)


def pair_block(hops, flip, own, other, b_own, b_other, cols, dtype=jnp.bfloat16):
    return pl.pallas_call(
        functools.partial(pair_kernel, hops, flip),
        out_shape=jax.ShapeDtypeStruct((ROWS, cols, LANES), dtype),
        in_specs=[WHOLE] * 4,
        out_specs=WHOLE,
        scratch_shapes=[pltpu.VMEM((FEATS * FEATS, ROWS * LANES), jnp.bfloat16)],
        compiler_params=limit(16),
        cost_estimate=cost(4 << 20, 3 << 30),
        name="pair_block",
    )(own, other, b_own, b_other)


def add_kernel(kept_ref, came_ref, out_ref):
    out_ref[...] = (kept_ref[...] + came_ref[...].astype(jnp.float32)).astype(out_ref.dtype)


def add_to(kept, came, dtype, name, nbytes):
    return pl.pallas_call(
        add_kernel,
        out_shape=jax.ShapeDtypeStruct(kept.shape, dtype),
        in_specs=[WHOLE, WHOLE],
        out_specs=WHOLE,
        compiler_params=limit(8),
        cost_estimate=cost(nbytes),
        name=name,
    )(kept, came)


def send(part, hops, flip=0):
    pairs = []
    for z in range(RING):
        for c in range(2):
            pairs.append((z * 2 + c, (z + hops[c]) % RING * 2 + (c ^ flip)))
    return lax.ppermute(part, DEPTH_AXES, pairs)


def local(first, second, matrix, bias):
    sequences = first.shape[0] * 2 * RING
    at = jnp.transpose(first, (1, 2, 0))
    bt = jnp.transpose(second, (1, 2, 0))
    cols = bt.shape[0]
    copies = spread(at)
    b_swapped = lax.ppermute(bt, "core", SWAP)
    a_own = lax.all_to_all(copies, TILE_AXES, split_axis=0, concat_axis=0, tiled=True)
    a_own = a_own.reshape(RING, 2, ROWS, FEATS, LANES)
    b_own = turn_own(bt, matrix)
    b_other = turn_other(b_swapped)
    a_swap, _ = lax.optimization_barrier((a_own, b_other))
    a_other = lax.ppermute(a_swap, "core", SWAP)
    block = functools.partial(
        pair_block, own=a_own, other=a_other, b_own=b_own, b_other=b_other, cols=cols
    )
    far = send(block((2, 2), False), (1, 3))
    left_part = block((1, 3), False, dtype=jnp.float32)
    right = send(block((1, 3), True), (1, 3), 1)
    kept = block((0, 0), False, dtype=jnp.float32)
    far, kept, left_part = lax.optimization_barrier((far, kept, left_part))
    merged = add_to(left_part, far, jnp.bfloat16, "merge", 200 << 20)
    left = send(merged, (1, 3))
    total = add_to(kept, right, jnp.float32, "presum", 200 << 20) + left.astype(jnp.float32)
    return (total * (1.0 / sequences) + bias).astype(jnp.bfloat16)


def solution(mesh):
    fine = Mesh(mesh.devices.reshape(RING, 2, 2, 4, 4), DEPTH_AXES + TILE_AXES)
    in_specs = (P(DEPTH_AXES, TILE_AXES, None), P(DEPTH_AXES, TILE_AXES, None), P(), P())
    out_specs = P(DEPTH_AXES, TILE_AXES, None)
    return jax.shard_map(local, mesh=fine, in_specs=in_specs, out_specs=out_specs, check_vma=False)
```

```python
import functools

import jax
import jax.numpy as jnp
from jax import lax
from jax.experimental import pallas as pl
from jax.experimental.pallas import tpu as pltpu
from jax.sharding import Mesh, PartitionSpec as P

FEATS = 32
ROWS = 8
LANES = 128
RING = 4
TILES = 32
DEPTH_AXES = ("zh", "core")
TILE_AXES = ("zl", "y", "x")
SWAP = [(0, 1), (1, 0)]
BLOCKS = (((2, 2), False), ((1, 3), False), ((1, 3), True), ((0, 0), False))
FAR, NEAR, CROSS, KEPT = range(4)
WHOLE = pl.BlockSpec(memory_space=pltpu.VMEM)
ANY = pl.BlockSpec(memory_space=pltpu.HBM)


def limit(mib):
    return pltpu.CompilerParams(vmem_limit_bytes=mib << 20)


def cost(nbytes, flops=0):
    return pl.CostEstimate(flops=flops, bytes_accessed=nbytes, transcendentals=0)


def spread_kernel(in_ref, out_ref, held_ref, filled_ref, in_sem, out_sem):
    fetch = pltpu.make_async_copy(in_ref, held_ref, in_sem)
    fetch.start()
    fetch.wait()
    own = held_ref[...]
    for t in range(TILES):
        filled_ref[t] = own
    store = pltpu.make_async_copy(filled_ref, out_ref, out_sem)
    store.start()
    store.wait()


def spread(own):
    return pl.pallas_call(
        spread_kernel,
        out_shape=jax.ShapeDtypeStruct((TILES,) + own.shape, jnp.bfloat16),
        in_specs=[ANY],
        out_specs=ANY,
        scratch_shapes=[
            pltpu.VMEM(own.shape, jnp.bfloat16),
            pltpu.VMEM((TILES,) + own.shape, jnp.bfloat16),
            pltpu.SemaphoreType.DMA,
            pltpu.SemaphoreType.DMA,
        ],
        compiler_params=limit(60),
        cost_estimate=cost(1 << 20),
        name="spread",
    )(own)


def turn(ref, wide_ref, out_ref):
    cols = ref.shape[0] // FEATS
    pad = jnp.zeros((LANES - cols, LANES), jnp.float32)
    wide_ref[...] = ref[...].astype(jnp.float32)
    for f in range(FEATS):
        picked = jnp.concatenate([wide_ref[pl.ds(f, cols, stride=FEATS), :], pad], axis=0)
        out_ref[0:LANES, f * LANES:(f + 1) * LANES] = picked.T.astype(jnp.bfloat16)


def matrix_kernel(matrix_ref, out_ref, wide_ref):
    wide_ref[...] = matrix_ref[...].astype(jnp.float32)
    group = LANES // FEATS
    for g in range(FEATS // group):
        rows = [wide_ref[pl.ds(g * group + i, FEATS, stride=FEATS), :] for i in range(group)]
        out_ref[:, g * LANES:(g + 1) * LANES] = jnp.concatenate(rows, axis=0).T.astype(
            jnp.bfloat16
        )


def turn_matrix(matrix):
    return pl.pallas_call(
        matrix_kernel,
        out_shape=jax.ShapeDtypeStruct((matrix.shape[1], matrix.shape[0]), jnp.bfloat16),
        scratch_shapes=[pltpu.VMEM(matrix.shape, jnp.float32)],
        in_specs=[WHOLE],
        out_specs=WHOLE,
        compiler_params=limit(8),
        cost_estimate=cost(2 << 20),
        name="turn_matrix",
    )(matrix)


def turn_kernel(b_ref, out_ref, wide_ref):
    turn(b_ref, wide_ref, out_ref)


def turn_factor(b):
    wide = (b.shape[0] * FEATS, LANES)
    return pl.pallas_call(
        turn_kernel,
        out_shape=jax.ShapeDtypeStruct((LANES, FEATS * LANES), jnp.bfloat16),
        scratch_shapes=[pltpu.VMEM(wide, jnp.float32)],
        in_specs=[WHOLE],
        out_specs=WHOLE,
        compiler_params=limit(8),
        cost_estimate=cost(4 << 20),
        name="turn_factor",
    )(b.reshape(wide))


def select_kernel(in_ref, out_ref):
    zh = lax.axis_index("zh")
    core = 1 - lax.axis_index("core")
    for slot, (hops, flip) in enumerate(BLOCKS):
        block = (zh + jnp.where(core == 0, hops[0], hops[1])) & (RING - 1)
        out_ref[slot] = in_ref[block, 1 - core if flip else core]


def select(a):
    return pl.pallas_call(
        select_kernel,
        out_shape=jax.ShapeDtypeStruct((len(BLOCKS),) + a.shape[2:], jnp.bfloat16),
        in_specs=[WHOLE],
        out_specs=WHOLE,
        compiler_params=limit(8),
        cost_estimate=cost(1 << 20),
        name="select",
    )(a)


def pair_kernel(slot, own_ref, other_ref, b_own_ref, b_other_ref, w_ref, out_ref, stack_ref):
    zh = lax.axis_index("zh")
    core = lax.axis_index("core")
    hops, flip = BLOCKS[slot]
    block = (zh + jnp.where(core == 0, hops[0], hops[1])) & (RING - 1)
    half = 1 - core if flip else core
    width = ROWS * FEATS
    a = jnp.concatenate(
        [
            own_ref[block, half].reshape(width, LANES),
            other_ref[slot].reshape(width, LANES),
        ],
        axis=1,
    )
    feats = 4
    for c in range(FEATS // feats):
        lanes = slice(c * feats * LANES, (c + 1) * feats * LANES)
        b = jnp.concatenate([b_own_ref[:, lanes], b_other_ref[:, lanes]], axis=0)
        outer = jnp.dot(a, b, preferred_element_type=jnp.float32).astype(jnp.bfloat16)
        for f in range(feats):
            k = (c * feats + f) * FEATS
            for r in range(ROWS):
                stack_ref[k:k + FEATS, r * LANES:(r + 1) * LANES] = outer[
                    r * FEATS:(r + 1) * FEATS, f * LANES:(f + 1) * LANES
                ]
    cols = out_ref.shape[1]
    for r in range(0, ROWS, 2):
        mixed = jnp.dot(
            w_ref[...], stack_ref[:, r * LANES:(r + 2) * LANES], preferred_element_type=jnp.float32
        )
        out_ref[r] = mixed[:, :LANES].T[:cols].astype(out_ref.dtype)
        out_ref[r + 1] = mixed[:, LANES:].T[:cols].astype(out_ref.dtype)


def pair_block(slot, own, other, b_own, b_other, wt, cols, dtype=jnp.bfloat16):
    return pl.pallas_call(
        functools.partial(pair_kernel, slot),
        out_shape=jax.ShapeDtypeStruct((ROWS, cols, LANES), dtype),
        in_specs=[WHOLE] * 5,
        out_specs=WHOLE,
        scratch_shapes=[pltpu.VMEM((FEATS * FEATS, ROWS * LANES), jnp.bfloat16)],
        compiler_params=limit(16),
        cost_estimate=cost(4 << 20, 3 << 30),
        name="pair_block",
    )(own, other, b_own, b_other, wt)


def add_kernel(kept_ref, came_ref, out_ref):
    out_ref[...] = (kept_ref[...] + came_ref[...].astype(jnp.float32)).astype(out_ref.dtype)


def add_to(kept, came, dtype, name, nbytes):
    return pl.pallas_call(
        add_kernel,
        out_shape=jax.ShapeDtypeStruct(kept.shape, dtype),
        in_specs=[WHOLE, WHOLE],
        out_specs=WHOLE,
        compiler_params=limit(8),
        cost_estimate=cost(nbytes),
        name=name,
    )(kept, came)


def send(part, hops, flip=0):
    pairs = []
    for z in range(RING):
        for c in range(2):
            pairs.append((z * 2 + c, (z + hops[c]) % RING * 2 + (c ^ flip)))
    return lax.ppermute(part, DEPTH_AXES, pairs)


def local(first, second, matrix, bias):
    sequences = first.shape[0] * 2 * RING
    at = jnp.transpose(first, (1, 2, 0))
    bt = jnp.transpose(second, (1, 2, 0))
    cols = bt.shape[0]
    copies = spread(at)
    b_swapped = lax.ppermute(bt, "core", SWAP)
    a_own = lax.all_to_all(copies, TILE_AXES, split_axis=0, concat_axis=0, tiled=True)
    a_own = a_own.reshape(RING, 2, ROWS, FEATS, LANES)
    b_own = turn_factor(bt)
    b_other = turn_factor(b_swapped)
    wt = turn_matrix(matrix)
    a_in, _, _ = lax.optimization_barrier((a_own, b_other, b_own))
    a_give = select(a_in)
    a_other = lax.ppermute(a_give, "core", SWAP)
    block = functools.partial(
        pair_block, own=a_own, other=a_other, b_own=b_own, b_other=b_other, wt=wt, cols=cols
    )
    far = send(block(FAR), (1, 3))
    left_part = block(NEAR, dtype=jnp.float32)
    right = send(block(CROSS), (1, 3), 1)
    kept = block(KEPT, dtype=jnp.float32)
    far, kept, left_part = lax.optimization_barrier((far, kept, left_part))
    merged = add_to(left_part, far, jnp.bfloat16, "merge", 200 << 20)
    left = send(merged, (1, 3))
    total = add_to(kept, right, jnp.float32, "presum", 200 << 20) + left.astype(jnp.float32)
    return (total * (1.0 / sequences) + bias).astype(jnp.bfloat16)


def solution(mesh):
    fine = Mesh(mesh.devices.reshape(RING, 2, 2, 4, 4), DEPTH_AXES + TILE_AXES)
    in_specs = (P(DEPTH_AXES, TILE_AXES, None), P(DEPTH_AXES, TILE_AXES, None), P(), P())
    out_specs = P(DEPTH_AXES, TILE_AXES, None)
    return jax.shard_map(local, mesh=fine, in_specs=in_specs, out_specs=out_specs, check_vma=False)
```

```python
import functools

import jax
import jax.numpy as jnp
from jax import lax
from jax.experimental import pallas as pl
from jax.experimental.pallas import tpu as pltpu
from jax.sharding import Mesh, PartitionSpec as P

FEATS = 32
ROWS = 8
LANES = 128
RING = 4
TILES = 32
DEPTH_AXES = ("zh", "core")
TILE_AXES = ("zl", "y", "x")
SWAP = [(0, 1), (1, 0)]
BLOCKS = (((2, 2), False), ((1, 3), False), ((1, 3), True), ((0, 0), False))
FAR, NEAR, CROSS, KEPT = range(4)
WHOLE = pl.BlockSpec(memory_space=pltpu.VMEM)
ANY = pl.BlockSpec(memory_space=pltpu.HBM)


def limit(mib):
    return pltpu.CompilerParams(vmem_limit_bytes=mib << 20)


def cost(nbytes, flops=0):
    return pl.CostEstimate(flops=flops, bytes_accessed=nbytes, transcendentals=0)


def spread_kernel(in_ref, out_ref, held_ref, filled_ref, in_sem, out_sems):
    fetch = pltpu.make_async_copy(in_ref, held_ref, in_sem)
    fetch.start()
    fetch.wait()
    own = held_ref[...]
    each = filled_ref.shape[0]
    for t in range(each):
        filled_ref[t] = own
    copies = [
        pltpu.make_async_copy(filled_ref, out_ref.at[pl.ds(i * each, each)], out_sems.at[i])
        for i in range(TILES // each)
    ]
    for copy in copies:
        copy.start()
    for copy in copies:
        copy.wait()


def spread(own):
    return pl.pallas_call(
        spread_kernel,
        out_shape=jax.ShapeDtypeStruct((TILES,) + own.shape, jnp.bfloat16),
        in_specs=[ANY],
        out_specs=ANY,
        scratch_shapes=[
            pltpu.VMEM(own.shape, jnp.bfloat16),
            pltpu.VMEM((8,) + own.shape, jnp.bfloat16),
            pltpu.SemaphoreType.DMA,
            pltpu.SemaphoreType.DMA((TILES // 8,)),
        ],
        compiler_params=limit(60),
        cost_estimate=cost(1 << 20),
        name="spread",
    )(own)


def turn(ref, wide_ref, out_ref):
    cols = ref.shape[0] // FEATS
    pad = jnp.zeros((LANES - cols, LANES), jnp.float32)
    wide_ref[...] = ref[...].astype(jnp.float32)
    for f in range(FEATS):
        picked = jnp.concatenate([wide_ref[pl.ds(f, cols, stride=FEATS), :], pad], axis=0)
        out_ref[0:LANES, f * LANES:(f + 1) * LANES] = picked.T.astype(jnp.bfloat16)


def matrix_kernel(matrix_ref, out_ref, wide_ref):
    wide_ref[...] = matrix_ref[...].astype(jnp.float32)
    group = LANES // FEATS
    for g in range(FEATS // group):
        rows = [wide_ref[pl.ds(g * group + i, FEATS, stride=FEATS), :] for i in range(group)]
        out_ref[:, g * LANES:(g + 1) * LANES] = jnp.concatenate(rows, axis=0).T.astype(
            jnp.bfloat16
        )


def turn_matrix(matrix):
    return pl.pallas_call(
        matrix_kernel,
        out_shape=jax.ShapeDtypeStruct((matrix.shape[1], matrix.shape[0]), jnp.bfloat16),
        scratch_shapes=[pltpu.VMEM(matrix.shape, jnp.float32)],
        in_specs=[WHOLE],
        out_specs=WHOLE,
        compiler_params=limit(8),
        cost_estimate=cost(2 << 20),
        name="turn_matrix",
    )(matrix)


def turn_kernel(b_ref, out_ref, wide_ref):
    turn(b_ref, wide_ref, out_ref)


def turn_factor(b):
    wide = (b.shape[0] * FEATS, LANES)
    return pl.pallas_call(
        turn_kernel,
        out_shape=jax.ShapeDtypeStruct((LANES, FEATS * LANES), jnp.bfloat16),
        scratch_shapes=[pltpu.VMEM(wide, jnp.float32)],
        in_specs=[WHOLE],
        out_specs=WHOLE,
        compiler_params=limit(8),
        cost_estimate=cost(4 << 20),
        name="turn_factor",
    )(b.reshape(wide))


def select_kernel(in_ref, out_ref):
    zh = lax.axis_index("zh")
    core = 1 - lax.axis_index("core")
    for slot, (hops, flip) in enumerate(BLOCKS):
        block = (zh + jnp.where(core == 0, hops[0], hops[1])) & (RING - 1)
        out_ref[slot] = in_ref[block, 1 - core if flip else core]


def select(a):
    return pl.pallas_call(
        select_kernel,
        out_shape=jax.ShapeDtypeStruct((len(BLOCKS),) + a.shape[2:], jnp.bfloat16),
        in_specs=[WHOLE],
        out_specs=WHOLE,
        compiler_params=limit(8),
        cost_estimate=cost(1 << 20),
        name="select",
    )(a)


def pair_kernel(slot, own_ref, other_ref, b_own_ref, b_other_ref, w_ref, out_ref, stack_ref):
    zh = lax.axis_index("zh")
    core = lax.axis_index("core")
    hops, flip = BLOCKS[slot]
    block = (zh + jnp.where(core == 0, hops[0], hops[1])) & (RING - 1)
    half = 1 - core if flip else core
    width = ROWS * FEATS
    a = jnp.concatenate(
        [
            own_ref[block, half].reshape(width, LANES),
            other_ref[slot].reshape(width, LANES),
        ],
        axis=1,
    )
    feats = 4
    for c in range(FEATS // feats):
        lanes = slice(c * feats * LANES, (c + 1) * feats * LANES)
        b = jnp.concatenate([b_own_ref[:, lanes], b_other_ref[:, lanes]], axis=0)
        outer = jnp.dot(a, b, preferred_element_type=jnp.float32).astype(jnp.bfloat16)
        for f in range(feats):
            k = (c * feats + f) * FEATS
            for r in range(ROWS):
                stack_ref[k:k + FEATS, r * LANES:(r + 1) * LANES] = outer[
                    r * FEATS:(r + 1) * FEATS, f * LANES:(f + 1) * LANES
                ]
    cols = out_ref.shape[1]
    for r in range(0, ROWS, 4):
        mixed = jnp.dot(
            w_ref[...], stack_ref[:, r * LANES:(r + 4) * LANES], preferred_element_type=jnp.float32
        )
        for i in range(4):
            lanes = slice(i * LANES, (i + 1) * LANES)
            out_ref[r + i] = mixed[:, lanes].T[:cols].astype(out_ref.dtype)


def pair_block(slot, own, other, b_own, b_other, wt, cols, dtype=jnp.bfloat16):
    return pl.pallas_call(
        functools.partial(pair_kernel, slot),
        out_shape=jax.ShapeDtypeStruct((ROWS, cols, LANES), dtype),
        in_specs=[WHOLE] * 5,
        out_specs=WHOLE,
        scratch_shapes=[pltpu.VMEM((FEATS * FEATS, ROWS * LANES), jnp.bfloat16)],
        compiler_params=limit(16),
        cost_estimate=cost(4 << 20, 3 << 30),
        name="pair_block",
    )(own, other, b_own, b_other, wt)


def add_kernel(kept_ref, came_ref, out_ref):
    out_ref[...] = (kept_ref[...] + came_ref[...].astype(jnp.float32)).astype(out_ref.dtype)


def add_to(kept, came, dtype, name, nbytes):
    return pl.pallas_call(
        add_kernel,
        out_shape=jax.ShapeDtypeStruct(kept.shape, dtype),
        in_specs=[WHOLE, WHOLE],
        out_specs=WHOLE,
        compiler_params=limit(8),
        cost_estimate=cost(nbytes),
        name=name,
    )(kept, came)


def final_kernel(scale, sum_ref, came_ref, bias_ref, out_ref, held_ref, sems):
    rows = sum_ref.shape[0]
    step = rows // sems.shape[0]
    bias = bias_ref[...]
    copies = []
    for i in range(sems.shape[0]):
        part = pl.ds(i * step, step)
        total = sum_ref[part] + came_ref[part].astype(jnp.float32)
        held_ref[part] = (total * scale + bias).astype(jnp.bfloat16)
        copies.append(pltpu.make_async_copy(held_ref.at[part], out_ref.at[part], sems.at[i]))
        copies[-1].start()
    for copy in copies:
        copy.wait()


def finish(kept, came, bias, scale):
    return pl.pallas_call(
        functools.partial(final_kernel, scale),
        out_shape=jax.ShapeDtypeStruct(kept.shape, jnp.bfloat16),
        in_specs=[WHOLE, WHOLE, WHOLE],
        out_specs=ANY,
        scratch_shapes=[
            pltpu.VMEM(kept.shape, jnp.bfloat16),
            pltpu.SemaphoreType.DMA((4,)),
        ],
        compiler_params=limit(4),
        cost_estimate=cost(1 << 20),
        name="finish",
    )(kept, came, bias.reshape(1, 1, LANES))


def send(part, hops, flip=0):
    pairs = []
    for z in range(RING):
        for c in range(2):
            pairs.append((z * 2 + c, (z + hops[c]) % RING * 2 + (c ^ flip)))
    return lax.ppermute(part, DEPTH_AXES, pairs)


def local(first, second, matrix, bias):
    sequences = first.shape[0] * 2 * RING
    at = jnp.transpose(first, (1, 2, 0))
    bt = jnp.transpose(second, (1, 2, 0))
    cols = bt.shape[0]
    copies = spread(at)
    b_swapped = lax.ppermute(bt, "core", SWAP)
    a_own = lax.all_to_all(copies, TILE_AXES, split_axis=0, concat_axis=0, tiled=True)
    a_own = a_own.reshape(RING, 2, ROWS, FEATS, LANES)
    b_own = turn_factor(bt)
    b_other = turn_factor(b_swapped)
    wt = turn_matrix(matrix)
    a_in, _, _ = lax.optimization_barrier((a_own, b_other, b_own))
    a_give = select(a_in)
    a_other = lax.ppermute(a_give, "core", SWAP)
    block = functools.partial(
        pair_block, own=a_own, other=a_other, b_own=b_own, b_other=b_other, wt=wt, cols=cols
    )
    far = send(block(FAR), (1, 3))
    left_part = block(NEAR, dtype=jnp.float32)
    right = send(block(CROSS), (1, 3), 1)
    kept = block(KEPT, dtype=jnp.float32)
    far, kept, left_part = lax.optimization_barrier((far, kept, left_part))
    merged = add_to(left_part, far, jnp.bfloat16, "merge", 200 << 20)
    left = send(merged, (1, 3))
    presum = add_to(kept, right, jnp.float32, "presum", 200 << 20)
    total = presum + left.astype(jnp.float32)
    return (total * (1.0 / sequences) + bias).astype(jnp.bfloat16)


def solution(mesh):
    fine = Mesh(mesh.devices.reshape(RING, 2, 2, 4, 4), DEPTH_AXES + TILE_AXES)
    in_specs = (P(DEPTH_AXES, TILE_AXES, None), P(DEPTH_AXES, TILE_AXES, None), P(), P())
    out_specs = P(DEPTH_AXES, TILE_AXES, None)
    return jax.shard_map(local, mesh=fine, in_specs=in_specs, out_specs=out_specs, check_vma=False)
```

```python
import functools

import jax
import jax.numpy as jnp
from jax import lax
from jax.experimental import pallas as pl
from jax.experimental.pallas import tpu as pltpu
from jax.sharding import Mesh, PartitionSpec as P

FEATS = 32
ROWS = 8
LANES = 128
RING = 4
TILES = 32
DEPTH_AXES = ("zh", "core")
TILE_AXES = ("zl", "y", "x")
SWAP = [(0, 1), (1, 0)]
BLOCKS = (((2, 2), False), ((1, 3), False), ((1, 3), True), ((0, 0), False))
FAR, NEAR, CROSS, KEPT = range(4)
WHOLE = pl.BlockSpec(memory_space=pltpu.VMEM)
ANY = pl.BlockSpec(memory_space=pltpu.HBM)


def limit(mib):
    return pltpu.CompilerParams(vmem_limit_bytes=mib << 20)


def cost(nbytes, flops=0):
    return pl.CostEstimate(flops=flops, bytes_accessed=nbytes, transcendentals=0)


def spread_kernel(in_ref, out_ref, held_ref, filled_ref, in_sem, out_sem):
    fetch = pltpu.make_async_copy(in_ref, held_ref, in_sem)
    fetch.start()
    fetch.wait()
    own = held_ref[...]
    for t in range(TILES):
        filled_ref[t] = own
    store = pltpu.make_async_copy(filled_ref, out_ref, out_sem)
    store.start()
    store.wait()


def spread(own):
    return pl.pallas_call(
        spread_kernel,
        out_shape=jax.ShapeDtypeStruct((TILES,) + own.shape, jnp.bfloat16),
        in_specs=[ANY],
        out_specs=ANY,
        scratch_shapes=[
            pltpu.VMEM(own.shape, jnp.bfloat16),
            pltpu.VMEM((TILES,) + own.shape, jnp.bfloat16),
            pltpu.SemaphoreType.DMA,
            pltpu.SemaphoreType.DMA,
        ],
        compiler_params=limit(60),
        cost_estimate=cost(1 << 20),
        name="spread",
    )(own)


def turn(ref, wide_ref, out_ref):
    cols = ref.shape[0] // FEATS
    pad = jnp.zeros((LANES - cols, LANES), jnp.float32)
    wide_ref[...] = ref[...].astype(jnp.float32)
    for f in range(FEATS):
        picked = jnp.concatenate([wide_ref[pl.ds(f, cols, stride=FEATS), :], pad], axis=0)
        out_ref[0:LANES, f * LANES:(f + 1) * LANES] = picked.T.astype(jnp.bfloat16)


def matrix_kernel(matrix_ref, out_ref, wide_ref):
    wide_ref[...] = matrix_ref[...].astype(jnp.float32)
    group = LANES // FEATS
    for g in range(FEATS // group):
        rows = [wide_ref[pl.ds(g * group + i, FEATS, stride=FEATS), :] for i in range(group)]
        out_ref[:, g * LANES:(g + 1) * LANES] = jnp.concatenate(rows, axis=0).T.astype(
            jnp.bfloat16
        )


def turn_matrix(matrix):
    return pl.pallas_call(
        matrix_kernel,
        out_shape=jax.ShapeDtypeStruct((matrix.shape[1], matrix.shape[0]), jnp.bfloat16),
        scratch_shapes=[pltpu.VMEM(matrix.shape, jnp.float32)],
        in_specs=[WHOLE],
        out_specs=WHOLE,
        compiler_params=limit(8),
        cost_estimate=cost(2 << 20),
        name="turn_matrix",
    )(matrix)


def turn_kernel(b_ref, out_ref, wide_ref):
    turn(b_ref, wide_ref, out_ref)


def turn_factor(b):
    wide = (b.shape[0] * FEATS, LANES)
    return pl.pallas_call(
        turn_kernel,
        out_shape=jax.ShapeDtypeStruct((LANES, FEATS * LANES), jnp.bfloat16),
        scratch_shapes=[pltpu.VMEM(wide, jnp.float32)],
        in_specs=[WHOLE],
        out_specs=WHOLE,
        compiler_params=limit(8),
        cost_estimate=cost(4 << 20),
        name="turn_factor",
    )(b.reshape(wide))


def select_kernel(in_ref, out_ref):
    zh = lax.axis_index("zh")
    core = 1 - lax.axis_index("core")
    for slot, (hops, flip) in enumerate(BLOCKS):
        block = (zh + jnp.where(core == 0, hops[0], hops[1])) & (RING - 1)
        out_ref[slot] = in_ref[block, 1 - core if flip else core]


def select(a):
    return pl.pallas_call(
        select_kernel,
        out_shape=jax.ShapeDtypeStruct((len(BLOCKS),) + a.shape[2:], jnp.bfloat16),
        in_specs=[WHOLE],
        out_specs=WHOLE,
        compiler_params=limit(8),
        cost_estimate=cost(1 << 20),
        name="select",
    )(a)


def pair_kernel(slot, own_ref, other_ref, b_own_ref, b_other_ref, w_ref, out_ref, stack_ref):
    zh = lax.axis_index("zh")
    core = lax.axis_index("core")
    hops, flip = BLOCKS[slot]
    block = (zh + jnp.where(core == 0, hops[0], hops[1])) & (RING - 1)
    half = 1 - core if flip else core
    width = ROWS * FEATS
    a = jnp.concatenate(
        [
            own_ref[block, half].reshape(width, LANES),
            other_ref[slot].reshape(width, LANES),
        ],
        axis=1,
    )
    feats = 4
    for c in range(FEATS // feats):
        lanes = slice(c * feats * LANES, (c + 1) * feats * LANES)
        b = jnp.concatenate([b_own_ref[:, lanes], b_other_ref[:, lanes]], axis=0)
        outer = jnp.dot(a, b, preferred_element_type=jnp.float32).astype(jnp.bfloat16)
        for f in range(feats):
            k = (c * feats + f) * FEATS
            for r in range(ROWS):
                stack_ref[k:k + FEATS, r * LANES:(r + 1) * LANES] = outer[
                    r * FEATS:(r + 1) * FEATS, f * LANES:(f + 1) * LANES
                ]
    cols = out_ref.shape[1]
    for r in range(0, ROWS, 2):
        mixed = jnp.dot(
            w_ref[...], stack_ref[:, r * LANES:(r + 2) * LANES], preferred_element_type=jnp.float32
        )
        out_ref[r] = mixed[:, :LANES].T[:cols].astype(out_ref.dtype)
        out_ref[r + 1] = mixed[:, LANES:].T[:cols].astype(out_ref.dtype)


def pair_block(slot, own, other, b_own, b_other, wt, cols, dtype=jnp.bfloat16):
    return pl.pallas_call(
        functools.partial(pair_kernel, slot),
        out_shape=jax.ShapeDtypeStruct((ROWS, cols, LANES), dtype),
        in_specs=[WHOLE] * 5,
        out_specs=WHOLE,
        scratch_shapes=[pltpu.VMEM((FEATS * FEATS, ROWS * LANES), jnp.bfloat16)],
        compiler_params=limit(16),
        cost_estimate=cost(1 << 16, 1 << 24),
        name="pair_block",
    )(own, other, b_own, b_other, wt)


def add_kernel(kept_ref, came_ref, out_ref):
    out_ref[...] = (kept_ref[...] + came_ref[...].astype(jnp.float32)).astype(out_ref.dtype)


def add_to(kept, came, dtype, name, nbytes):
    return pl.pallas_call(
        add_kernel,
        out_shape=jax.ShapeDtypeStruct(kept.shape, dtype),
        in_specs=[WHOLE, WHOLE],
        out_specs=WHOLE,
        compiler_params=limit(8),
        cost_estimate=cost(nbytes),
        name=name,
    )(kept, came)


def final_kernel(scale, sum_ref, came_ref, bias_ref, out_ref, held_ref, sems):
    rows = sum_ref.shape[0]
    step = rows // sems.shape[0]
    bias = bias_ref[...]
    copies = []
    for i in range(sems.shape[0]):
        part = pl.ds(i * step, step)
        total = sum_ref[part] + came_ref[part].astype(jnp.float32)
        held_ref[part] = (total * scale + bias).astype(jnp.bfloat16)
        copies.append(pltpu.make_async_copy(held_ref.at[part], out_ref.at[part], sems.at[i]))
        copies[-1].start()
    for copy in copies:
        copy.wait()


def finish(kept, came, bias, scale):
    return pl.pallas_call(
        functools.partial(final_kernel, scale),
        out_shape=jax.ShapeDtypeStruct(kept.shape, jnp.bfloat16),
        in_specs=[WHOLE, WHOLE, WHOLE],
        out_specs=ANY,
        scratch_shapes=[
            pltpu.VMEM(kept.shape, jnp.bfloat16),
            pltpu.SemaphoreType.DMA((4,)),
        ],
        compiler_params=limit(4),
        cost_estimate=cost(1 << 20),
        name="finish",
    )(kept, came, bias.reshape(1, 1, LANES))


def send(part, hops, flip=0):
    pairs = []
    for z in range(RING):
        for c in range(2):
            pairs.append((z * 2 + c, (z + hops[c]) % RING * 2 + (c ^ flip)))
    return lax.ppermute(part, DEPTH_AXES, pairs)


def local(first, second, matrix, bias):
    sequences = first.shape[0] * 2 * RING
    at = jnp.transpose(first, (1, 2, 0))
    bt = jnp.transpose(second, (1, 2, 0))
    cols = bt.shape[0]
    copies = spread(at)
    b_swapped = lax.ppermute(bt, "core", SWAP)
    a_own = lax.all_to_all(copies, TILE_AXES, split_axis=0, concat_axis=0, tiled=True)
    a_own = a_own.reshape(RING, 2, ROWS, FEATS, LANES)
    b_own = turn_factor(bt)
    b_other = turn_factor(b_swapped)
    wt = turn_matrix(matrix)
    a_in, _, _ = lax.optimization_barrier((a_own, b_other, b_own))
    a_give = select(a_in)
    a_other = lax.ppermute(a_give, "core", SWAP)
    block = functools.partial(
        pair_block, own=a_own, other=a_other, b_own=b_own, b_other=b_other, wt=wt, cols=cols
    )
    far = send(block(FAR), (1, 3))
    left_part = block(NEAR, dtype=jnp.float32)
    right = send(block(CROSS), (1, 3), 1)
    kept = block(KEPT, dtype=jnp.float32)
    far, left_part = lax.optimization_barrier((far, left_part))
    merged = add_to(left_part, far, jnp.bfloat16, "merge", 200 << 20)
    left = send(merged, (1, 3))
    presum = add_to(kept, right, jnp.float32, "presum", 200 << 20)
    total = presum + left.astype(jnp.float32)
    return (total * (1.0 / sequences) + bias).astype(jnp.bfloat16)


def solution(mesh):
    fine = Mesh(mesh.devices.reshape(RING, 2, 2, 4, 4), DEPTH_AXES + TILE_AXES)
    in_specs = (P(DEPTH_AXES, TILE_AXES, None), P(DEPTH_AXES, TILE_AXES, None), P(), P())
    out_specs = P(DEPTH_AXES, TILE_AXES, None)
    return jax.shard_map(local, mesh=fine, in_specs=in_specs, out_specs=out_specs, check_vma=False)
```

```python
import functools

import jax
import jax.numpy as jnp
from jax import lax
from jax.experimental import pallas as pl
from jax.experimental.pallas import tpu as pltpu
from jax.sharding import Mesh, PartitionSpec as P

FEATS = 32
ROWS = 8
LANES = 128
RING = 4
TILES = 32
DEPTH_AXES = ("zh", "core")
TILE_AXES = ("zl", "y", "x")
SWAP = [(0, 1), (1, 0)]
BLOCKS = (((2, 2), False), ((1, 3), False), ((1, 3), True), ((0, 0), False))
FAR, NEAR, CROSS, KEPT = range(4)
WHOLE = pl.BlockSpec(memory_space=pltpu.VMEM)
ANY = pl.BlockSpec(memory_space=pltpu.HBM)


def limit(mib):
    return pltpu.CompilerParams(vmem_limit_bytes=mib << 20)


def cost(nbytes, flops=0):
    return pl.CostEstimate(flops=flops, bytes_accessed=nbytes, transcendentals=0)


def spread_kernel(in_ref, out_ref, held_ref, filled_ref, in_sem, out_sem):
    fetch = pltpu.make_async_copy(in_ref, held_ref, in_sem)
    fetch.start()
    fetch.wait()
    own = held_ref[...]
    for t in range(TILES):
        filled_ref[t] = own
    store = pltpu.make_async_copy(filled_ref, out_ref, out_sem)
    store.start()
    store.wait()


def spread(own):
    return pl.pallas_call(
        spread_kernel,
        out_shape=jax.ShapeDtypeStruct((TILES,) + own.shape, jnp.bfloat16),
        in_specs=[ANY],
        out_specs=ANY,
        scratch_shapes=[
            pltpu.VMEM(own.shape, jnp.bfloat16),
            pltpu.VMEM((TILES,) + own.shape, jnp.bfloat16),
            pltpu.SemaphoreType.DMA,
            pltpu.SemaphoreType.DMA,
        ],
        compiler_params=limit(60),
        cost_estimate=cost(1 << 20),
        name="spread",
    )(own)


def turn(ref, wide_ref, out_ref):
    cols = ref.shape[0] // FEATS
    pad = jnp.zeros((LANES - cols, LANES), jnp.float32)
    wide_ref[...] = ref[...].astype(jnp.float32)
    for f in range(FEATS):
        picked = jnp.concatenate([wide_ref[pl.ds(f, cols, stride=FEATS), :], pad], axis=0)
        out_ref[0:LANES, f * LANES:(f + 1) * LANES] = picked.T.astype(jnp.bfloat16)


def matrix_kernel(matrix_ref, out_ref, wide_ref):
    wide_ref[...] = matrix_ref[...].astype(jnp.float32)
    group = LANES // FEATS
    for g in range(FEATS // group):
        rows = [wide_ref[pl.ds(g * group + i, FEATS, stride=FEATS), :] for i in range(group)]
        out_ref[:, g * LANES:(g + 1) * LANES] = jnp.concatenate(rows, axis=0).T.astype(
            jnp.bfloat16
        )


def turn_matrix(matrix):
    return pl.pallas_call(
        matrix_kernel,
        out_shape=jax.ShapeDtypeStruct((matrix.shape[1], matrix.shape[0]), jnp.bfloat16),
        scratch_shapes=[pltpu.VMEM(matrix.shape, jnp.float32)],
        in_specs=[WHOLE],
        out_specs=WHOLE,
        compiler_params=limit(8),
        cost_estimate=cost(2 << 20),
        name="turn_matrix",
    )(matrix)


def turn_kernel(b_ref, out_ref, wide_ref):
    turn(b_ref, wide_ref, out_ref)


def turn_factor(b):
    wide = (b.shape[0] * FEATS, LANES)
    return pl.pallas_call(
        turn_kernel,
        out_shape=jax.ShapeDtypeStruct((LANES, FEATS * LANES), jnp.bfloat16),
        scratch_shapes=[pltpu.VMEM(wide, jnp.float32)],
        in_specs=[WHOLE],
        out_specs=WHOLE,
        compiler_params=limit(8),
        cost_estimate=cost(4 << 20),
        name="turn_factor",
    )(b.reshape(wide))


def select_kernel(in_ref, out_ref):
    zh = lax.axis_index("zh")
    core = 1 - lax.axis_index("core")
    for slot, (hops, flip) in enumerate(BLOCKS):
        block = (zh + jnp.where((core + lax.axis_index("zl")) & 1 == 0, hops[0], hops[1])) & (RING - 1)
        out_ref[slot] = in_ref[block, 1 - core if flip else core]


def select(a):
    return pl.pallas_call(
        select_kernel,
        out_shape=jax.ShapeDtypeStruct((len(BLOCKS),) + a.shape[2:], jnp.bfloat16),
        in_specs=[WHOLE],
        out_specs=WHOLE,
        compiler_params=limit(8),
        cost_estimate=cost(1 << 20),
        name="select",
    )(a)


def pair_kernel(slot, own_ref, other_ref, b_own_ref, b_other_ref, w_ref, out_ref, stack_ref):
    zh = lax.axis_index("zh")
    core = lax.axis_index("core")
    hops, flip = BLOCKS[slot]
    block = (zh + jnp.where((core + lax.axis_index("zl")) & 1 == 0, hops[0], hops[1])) & (RING - 1)
    half = 1 - core if flip else core
    width = ROWS * FEATS
    a = jnp.concatenate(
        [
            own_ref[block, half].reshape(width, LANES),
            other_ref[slot].reshape(width, LANES),
        ],
        axis=1,
    )
    feats = 4
    for c in range(FEATS // feats):
        lanes = slice(c * feats * LANES, (c + 1) * feats * LANES)
        b = jnp.concatenate([b_own_ref[:, lanes], b_other_ref[:, lanes]], axis=0)
        outer = jnp.dot(a, b, preferred_element_type=jnp.float32).astype(jnp.bfloat16)
        for f in range(feats):
            k = (c * feats + f) * FEATS
            for r in range(ROWS):
                stack_ref[k:k + FEATS, r * LANES:(r + 1) * LANES] = outer[
                    r * FEATS:(r + 1) * FEATS, f * LANES:(f + 1) * LANES
                ]
    cols = out_ref.shape[1]
    for r in range(0, ROWS, 2):
        mixed = jnp.dot(
            w_ref[...], stack_ref[:, r * LANES:(r + 2) * LANES], preferred_element_type=jnp.float32
        )
        out_ref[r] = mixed[:, :LANES].T[:cols].astype(out_ref.dtype)
        out_ref[r + 1] = mixed[:, LANES:].T[:cols].astype(out_ref.dtype)


def pair_block(slot, own, other, b_own, b_other, wt, cols, dtype=jnp.bfloat16):
    return pl.pallas_call(
        functools.partial(pair_kernel, slot),
        out_shape=jax.ShapeDtypeStruct((ROWS, cols, LANES), dtype),
        in_specs=[WHOLE] * 5,
        out_specs=WHOLE,
        scratch_shapes=[pltpu.VMEM((FEATS * FEATS, ROWS * LANES), jnp.bfloat16)],
        compiler_params=limit(16),
        cost_estimate=cost(4 << 20, 3 << 30),
        name="pair_block",
    )(own, other, b_own, b_other, wt)


def add_kernel(kept_ref, came_ref, out_ref):
    out_ref[...] = (kept_ref[...] + came_ref[...].astype(jnp.float32)).astype(out_ref.dtype)


def add_to(kept, came, dtype, name, nbytes):
    return pl.pallas_call(
        add_kernel,
        out_shape=jax.ShapeDtypeStruct(kept.shape, dtype),
        in_specs=[WHOLE, WHOLE],
        out_specs=WHOLE,
        compiler_params=limit(8),
        cost_estimate=cost(nbytes),
        name=name,
    )(kept, came)


def final_kernel(scale, sum_ref, came_ref, bias_ref, out_ref, held_ref, sems):
    rows = sum_ref.shape[0]
    step = rows // sems.shape[0]
    bias = bias_ref[...]
    copies = []
    for i in range(sems.shape[0]):
        part = pl.ds(i * step, step)
        total = sum_ref[part] + came_ref[part].astype(jnp.float32)
        held_ref[part] = (total * scale + bias).astype(jnp.bfloat16)
        copies.append(pltpu.make_async_copy(held_ref.at[part], out_ref.at[part], sems.at[i]))
        copies[-1].start()
    for copy in copies:
        copy.wait()


def finish(kept, came, bias, scale):
    return pl.pallas_call(
        functools.partial(final_kernel, scale),
        out_shape=jax.ShapeDtypeStruct(kept.shape, jnp.bfloat16),
        in_specs=[WHOLE, WHOLE, WHOLE],
        out_specs=ANY,
        scratch_shapes=[
            pltpu.VMEM(kept.shape, jnp.bfloat16),
            pltpu.SemaphoreType.DMA((4,)),
        ],
        compiler_params=limit(4),
        cost_estimate=cost(1 << 20),
        name="finish",
    )(kept, came, bias.reshape(1, 1, LANES))


def send(part, hops, flip=0):
    pairs = []
    for z in range(RING):
        for c in range(2):
            for low in range(2):
                to = (z + hops[c ^ low]) % RING
                pairs.append(((z * 2 + c) * 2 + low, (to * 2 + (c ^ flip)) * 2 + low))
    return lax.ppermute(part, DEPTH_AXES + ("zl",), pairs)


def local(first, second, matrix, bias):
    sequences = first.shape[0] * 2 * RING
    at = jnp.transpose(first, (1, 2, 0))
    bt = jnp.transpose(second, (1, 2, 0))
    cols = bt.shape[0]
    copies = spread(at)
    b_swapped = lax.ppermute(bt, "core", SWAP)
    a_own = lax.all_to_all(copies, TILE_AXES, split_axis=0, concat_axis=0, tiled=True)
    a_own = a_own.reshape(RING, 2, ROWS, FEATS, LANES)
    b_own = turn_factor(bt)
    b_other = turn_factor(b_swapped)
    wt = turn_matrix(matrix)
    a_in, _, _ = lax.optimization_barrier((a_own, b_other, b_own))
    a_give = select(a_in)
    a_other = lax.ppermute(a_give, "core", SWAP)
    block = functools.partial(
        pair_block, own=a_own, other=a_other, b_own=b_own, b_other=b_other, wt=wt, cols=cols
    )
    far = send(block(FAR), (1, 3))
    left_part = block(NEAR, dtype=jnp.float32)
    right = send(block(CROSS), (1, 3), 1)
    kept = block(KEPT, dtype=jnp.float32)
    far, kept, left_part = lax.optimization_barrier((far, kept, left_part))
    merged = add_to(left_part, far, jnp.bfloat16, "merge", 200 << 20)
    left = send(merged, (1, 3))
    presum = add_to(kept, right, jnp.float32, "presum", 200 << 20)
    total = presum + left.astype(jnp.float32)
    return (total * (1.0 / sequences) + bias).astype(jnp.bfloat16)


def solution(mesh):
    fine = Mesh(mesh.devices.reshape(RING, 2, 2, 4, 4), DEPTH_AXES + TILE_AXES)
    in_specs = (P(DEPTH_AXES, TILE_AXES, None), P(DEPTH_AXES, TILE_AXES, None), P(), P())
    out_specs = P(DEPTH_AXES, TILE_AXES, None)
    return jax.shard_map(local, mesh=fine, in_specs=in_specs, out_specs=out_specs, check_vma=False)
```
